256 devices in a mesh: item: 16 (over x, z_lo), store: 16 (over y, z_hi, core).
Axes of the slice: x: 4, y: 4, z: 8 (z_hi: 2, z_lo: 4; z = z_hi * 4 + z_lo), core: 2. Of those that a mesh axis runs over, the one named last changes fastest.
Arguments:
- sales: float32 [8, 16384, 4096], P(None, 'item', 'store'), may hold values from -6 to 6
- launch_week: int32 [16384], P('item'), may hold values from 0 to 8
- open_week: int32 [4096], P('store'), may hold values from 0 to 7
- item_factors: float32 [16384, 128], P(('item', 'store')), may hold values from -4 to 4
- store_factors: float32 [4096, 128], P(('store', 'item')), may hold values from -4 to 4
- week_factors: float32 [8, 128], replicated, may hold values from -4 to 4
Outputs:
- new_items: float32 [16384, 128], P(('item', 'store'))
- new_stores: float32 [4096, 128], P(('store', 'item'))
- new_weeks: float32 [8, 128], replicated
- losses: float32 [2], replicated
The draws below stay inside these ranges and needn't reach their ends.
All inputs are finite; a program needn't handle non-finite values.
Results may differ from the reference program's by a relative error of at most 0.0003.
Values sent between devices are 32-bit elements; how exact they have to be, the bound alone decides.
No kernel may reach another device: no remote copies, remote signals or barrier semaphores. Data moves between devices by JAX's collectives and lax.ppermute only.
A program may use at most 64 MiB of HBM per device.

```python
import jax
import jax.numpy as jnp
from jax import lax

R = 128
W = 8
STEPS = 2
NI = 16384
NS = 4096
N_ITEM = 16


def plant(values, key, smallest, largest):
    shape = values.shape
    index_at = [jax.random.randint(jax.random.fold_in(key, axis), (), 0, shape[axis]) for axis in range(len(shape))]
    values = values.at[tuple(index_at)].set(smallest)
    longest = shape.index(max(shape))
    index_at[longest] = (index_at[longest] + 1) % shape[longest]
    return values.at[tuple(index_at)].set(largest)


def block_levels(rng, shape, cuts, low, largest):
    level = 1.0
    for axis_at, parts in cuts:
        draws = jax.random.uniform(jax.random.fold_in(jax.random.fold_in(rng, 6), axis_at), (parts,), jnp.float32, low / len(cuts), largest / len(cuts))
        level = level * jnp.repeat(jnp.exp(draws), shape[axis_at] // parts).reshape((-1,) + (1,) * (len(shape) - 1 - axis_at))
    return level


def centred(stream_key, shape, scale, limit, shards=(), held_as=jnp.bfloat16):
    entries = scale * jax.random.normal(stream_key, shape, jnp.float32)
    if shards:
        entries = entries * block_levels(stream_key, shape, shards, -0.22, 0.18)
    return jnp.clip(entries, -limit, limit).astype(held_as)


def setup_inputs(seed: int = 0) -> dict:
    arg_keys = jax.random.split(jax.random.key(seed), 7)
    return {
        "sales": centred(arg_keys[0], (W, NI, NS), 1.0, 6.0, ((1, 16), (2, 16)), jnp.float32),
        "launch_week": plant(jax.random.randint(arg_keys[1], (NI,), 0, W + 1), jax.random.fold_in(arg_keys[1], 1), 0, W).astype(jnp.int32),
        "open_week": plant(jax.random.randint(arg_keys[2], (NS,), 0, W), jax.random.fold_in(arg_keys[2], 1), 0, W - 1).astype(jnp.int32),
        "item_factors": centred(arg_keys[3], (NI, R), 0.45, 4.0, ((0, 256),), jnp.float32),
        "store_factors": centred(arg_keys[4], (NS, R), 0.45, 4.0, ((0, 256),), jnp.float32),
        "week_factors": centred(arg_keys[5], (W, R), 0.45, 4.0, (), jnp.float32),
    }


def block_terms(values, rows_a, store_b, week_c, launch_rows, open_cols):
    weeks = jnp.arange(values.shape[0]).astype(jnp.int32)
    mask = ((weeks[:, None, None] >= launch_rows[None, :, None]) & (weeks[:, None, None] >= open_cols[None, None, :])).astype(jnp.float32)
    scaled = rows_a[None, :, :] * week_c[:, None, :]
    recon = jnp.einsum("wir,sr->wis", scaled, store_b, precision=lax.Precision.HIGHEST)
    error = mask * (recon - values)
    error_b = jnp.einsum("wis,sr->wir", error, store_b, precision=lax.Precision.HIGHEST)
    grad_a = jnp.sum(error_b * week_c[:, None, :], axis=0)
    grad_c = jnp.einsum("wir,ir->wr", error_b, rows_a, precision=lax.Precision.HIGHEST)
    grad_b = jnp.einsum("wis,wir->sr", error, scaled, precision=lax.Precision.HIGHEST)
    return grad_a, grad_b, grad_c, jnp.sum(error * error)


def reference(sales, launch_week, open_week, item_factors, store_factors, week_factors):
    block_rows = NI // N_ITEM
    count = NI * NS * W
    factor_a, factor_b, factor_c = item_factors, store_factors, week_factors
    loss_list = []
    for step in range(STEPS):
        def visit(carry, index):
            acc_b, acc_c, acc_sq = carry
            start = (index * block_rows).astype(jnp.int32)
            values = lax.dynamic_slice_in_dim(sales, start, block_rows, 1)
            rows_a = lax.dynamic_slice_in_dim(factor_a, start, block_rows, 0)
            launch_rows = lax.dynamic_slice_in_dim(launch_week, start, block_rows, 0)
            grad_a, grad_b, grad_c, square = block_terms(values, rows_a, factor_b, factor_c, launch_rows, open_week)
            return (acc_b + grad_b, acc_c + grad_c, acc_sq + square), grad_a

        start_carry = (jnp.zeros((NS, R), jnp.float32), jnp.zeros((W, R), jnp.float32), jnp.zeros((), jnp.float32))
        (grad_b, grad_c, square), grad_blocks = lax.scan(visit, start_carry, jnp.arange(N_ITEM).astype(jnp.int32))
        grad_a = grad_blocks.reshape(NI, R)
        loss_list.append(square / (2.0 * count))
        factor_a = factor_a - (40.0 / (NS * W)) * grad_a
        factor_b = factor_b - (40.0 / (NI * W)) * grad_b
        factor_c = factor_c - (40.0 / (NI * NS)) * grad_c
    return factor_a, factor_b, factor_c, jnp.stack(loss_list)
```

```python
import functools

import jax
import jax.numpy as jnp
from jax import lax
from jax.experimental import pallas as pl
from jax.experimental.pallas import tpu as pltpu
from jax.sharding import PartitionSpec as P

CORE, ZHI = 1, 2
OUTER = (4, 8, 12)
ZLOS = (1, 2, 3)
MIB = 1 << 20
LONG = 10**11
F32 = jnp.float32
BF16 = jnp.bfloat16
VM = pl.BlockSpec(memory_space=pltpu.VMEM)


def swap(value, axis, bits):
    return lax.ppermute(value, axis, [(i, i ^ bits) for i in range(16)])


def split(value):
    high = value.astype(BF16)
    return high, (value - high.astype(F32)).astype(BF16)


def row_of(axis, rows, bits):
    return pl.multiple_of((lax.axis_index(axis) ^ bits) * rows, rows)


def tree(values):
    while len(values) > 1:
        values = [a + b for a, b in zip(values[::2], values[1::2])]
    return values[0]


def small_call(kernel, outs, *args, flops=None, scratch=()):
    cost = pl.CostEstimate(flops=flops or 0, bytes_accessed=0, transcendentals=0)
    outs = [o if isinstance(o, jax.ShapeDtypeStruct) else jax.ShapeDtypeStruct(o, F32) for o in outs]
    return pl.pallas_call(
        kernel,
        out_shape=outs,
        in_specs=[VM] * len(args),
        out_specs=[VM] * len(outs),
        scratch_shapes=scratch,
        compiler_params=pltpu.CompilerParams(vmem_limit_bytes=8 * MIB),
        cost_estimate=cost,
    )(*args)


def step_kernel(sub, rate_c, riding, *refs):
    sales_ref, late_ref, b_ref, c_ref, old_weeks = refs[:5]
    rows_of = refs[5:7]
    er, gbt_ref, weeks_ref, newc_ref = refs[7:11]
    a_f, a3, at = refs[11:]
    weeks, n_items, n_stores = sales_ref.shape
    rank = a_f.shape[1]
    rows = 256

    for o in range(2):
        for d in range(4):
            for h in range(2):
                row = row_of("store", sub, 4 * d + 2 * h + o)
                a_f[pl.ds(row, sub), :] = rows_of[o][(2 * d + h) * sub : (2 * d + h + 1) * sub, :]
    a = a_f[...]
    high, low = split(a)
    a3[:, :rank] = high
    a3[:, rank : 2 * rank] = low
    a3[:, 2 * rank :] = high
    high, low = split(a.T)
    at[:rank, :] = high
    at[rank:, :] = low
    b = b_ref[...]
    bt = b.T
    c = c_ref[...]
    if riding:
        c = c - rate_c * rows_of[0][8 * sub :, :]
    newc_ref[...] = c

    def factor(w):
        high, low = split(b * c[w : w + 1, :])
        return jnp.concatenate([high, high, low], axis=1)

    def errors(w, i, bc3, total_s):
        part = slice(i * rows, (i + 1) * rows)
        recon = lax.dot_general(a3[part, :], bc3, (((1,), (1,)), ((), ())), preferred_element_type=F32)
        error = jnp.where(late_ref[part, :] <= w, recon - sales_ref[w, part, :], 0.0)
        er[w, part, :] = error.astype(BF16)
        return total_s + jnp.sum((error * error).reshape(rows // 8, 8, n_stores), axis=0)

    n = n_items // rows
    total_s = jnp.zeros((8, n_stores), F32)
    gbt = jnp.zeros((rank, n_stores), F32)
    week_columns = []
    bc3 = factor(0)
    for i in range(n):
        total_s = errors(0, i, bc3, total_s)
    for w in range(weeks):
        if w + 1 < weeks:
            bc3 = factor(w + 1)
            for i in range(n):
                total_s = errors(w + 1, i, bc3, total_s)
        x = jnp.dot(at[...], er[w], preferred_element_type=F32)
        x = x[:rank, :] + x[rank:, :]
        week_columns.append(jnp.sum(x * bt, axis=1, keepdims=True))
        turn = jnp.broadcast_to(c[w : w + 1, :], (rank, rank)).T
        gbt = gbt + jnp.concatenate([turn] * (n_stores // rank), axis=1) * x

    lane = lax.broadcasted_iota(jnp.int32, (rank, rank), 1)
    gc = jnp.zeros((rank, rank), F32)
    for w in range(weeks):
        gc = jnp.where(lane == w, week_columns[w], gc)
    gc = gc.T[:weeks, :]
    s = jnp.sum(total_s, axis=0, keepdims=True)
    loss = s[:, :rank]
    for i in range(1, n_stores // rank):
        loss = loss + s[:, i * rank : (i + 1) * rank]
    at_row = lax.broadcasted_iota(jnp.int32, (8, rank), 0)
    losses = jnp.where(at_row == int(riding), loss, old_weeks[weeks:, :])
    gbt_ref[...] = gbt
    weeks_ref[:weeks, :] = gc
    weeks_ref[weeks:, :] = losses


def step_call(sub, rate_c, riding, sales, late, block_b, factor_c, old_weeks, mine, other):
    weeks, n_items, n_stores = sales.shape
    rank = block_b.shape[1]
    outs = [(rank, n_stores), (weeks + 8, rank), (weeks, rank)]
    args = [sales, late, block_b, factor_c, old_weeks, mine, other]
    return pl.pallas_call(
        functools.partial(step_kernel, sub, rate_c, riding),
        out_shape=[jax.ShapeDtypeStruct(sales.shape, BF16)] + [jax.ShapeDtypeStruct(s, F32) for s in outs],
        in_specs=[VM] * len(args),
        out_specs=[VM] * (1 + len(outs)),
        scratch_shapes=[
            pltpu.VMEM((n_items, rank), F32),
            pltpu.VMEM((n_items, 3 * rank), BF16),
            pltpu.VMEM((2 * rank, n_items), BF16),
        ],
        compiler_params=pltpu.CompilerParams(vmem_limit_bytes=28 * MIB),
        cost_estimate=pl.CostEstimate(
            flops=4 * n_items * n_stores * weeks * rank, bytes_accessed=4 * n_items * n_stores * weeks, transcendentals=0
        ),
    )(*args)


def items_grad_kernel(er, b_ref, c_ref, after_ref, send_ref, own_ref, ga):
    weeks, n_items, n_stores = er.shape
    rank = b_ref.shape[1]
    rows = 256
    b = b_ref[...]
    factors = [jnp.concatenate(split(b * c_ref[w : w + 1, :]), axis=1) for w in range(weeks)]
    for i in range(n_items // rows):
        part = slice(i * rows, (i + 1) * rows)
        g = jnp.dot(er[0, part, :], factors[0], preferred_element_type=F32)
        for w in range(1, weeks):
            g = g + jnp.dot(er[w, part, :], factors[w], preferred_element_type=F32)
        ga[part, :] = g[:, :rank] + g[:, rank:]
    sub = send_ref.shape[0] // 8
    for other, out in ((0, own_ref), (1, send_ref)):
        for d in range(4):
            for h in range(2):
                row = row_of("store", sub, 4 * d + 2 * h + other)
                out[(d * 2 + h) * sub : (d * 2 + h + 1) * sub, :] = ga[pl.ds(row, sub), :]


def items_grad_call(er, block_b, factor_c, after):
    weeks, n_items, n_stores = er.shape
    rank = block_b.shape[1]
    return pl.pallas_call(
        items_grad_kernel,
        out_shape=[jax.ShapeDtypeStruct((n_items // 2, rank), F32)] * 2,
        in_specs=[VM] * 4,
        out_specs=[VM] * 2,
        scratch_shapes=[pltpu.VMEM((n_items, rank), F32)],
        compiler_params=pltpu.CompilerParams(vmem_limit_bytes=16 * MIB),
        cost_estimate=pl.CostEstimate(flops=0, bytes_accessed=0, transcendentals=0),
    )(er, block_b, factor_c, after)


def prepare_kernel(a_hbm, b_hbm, launch_hbm, open_hbm, own_ref, b_ref, late_ref, launch_ref, open_ref, sems):
    pairs = ((b_hbm, b_ref), (launch_hbm, launch_ref), (open_hbm, open_ref), (a_hbm, own_ref))
    copies = [pltpu.make_async_copy(x, y, sems.at[k]) for k, (x, y) in enumerate(pairs)]
    for copy in copies:
        copy.start()
    for copy in copies:
        copy.wait()
    lanes = launch_ref.shape[1]
    opened = open_ref[...]
    for k in range(launch_ref.shape[0]):
        turned = jnp.broadcast_to(launch_ref[k : k + 1, :], (lanes, lanes)).T
        for j in range(opened.shape[1] // lanes):
            part = slice(j * lanes, (j + 1) * lanes)
            late_ref[k * lanes : (k + 1) * lanes, part] = jnp.maximum(turned, opened[:, part])


def join_kernel(own_ref, other_ref, b0, b1, b2, b3, a_out, b_out):
    sub, share = own_ref.shape[0], b0.shape[0]
    a_out[:sub, :] = own_ref[...]
    a_out[sub:, :] = other_ref[...]
    for d, ref in enumerate((b0, b1, b2, b3)):
        b_out[d * share : (d + 1) * share, :] = ref[...]


def assemble_kernel(w0, w1, w2, w3, q0, q1, q2, q3, items_ref, b_ref):
    rows = items_ref.shape[0] // 32 * 8
    for d, ref in enumerate((w0, w1, w2, w3)):
        items_ref[d * rows : (d + 1) * rows, :] = ref[:rows, :]
    if w0.shape[0] > rows:
        items_ref[4 * rows :, :] = (w0[rows:, :] + w1[rows:, :]) + (w2[rows:, :] + w3[rows:, :])
    place_stores((q0, q1, q2, q3), b_ref)


def place_stores(quarters, out_ref):
    share = out_ref.shape[0] // 16
    for e, ref in enumerate(quarters):
        for d in range(4):
            out_ref[pl.ds(row_of("item", share, 4 * e + d), share), :] = ref[d * share : (d + 1) * share, :]


def pack_kernel(used, gbt_ref, mine_ref, core_ref, *refs):
    outs, gb = refs[:4], refs[4]
    gb[...] = gbt_ref[...].T
    share = gb.shape[0] // 16
    more = used - 4 * share
    for e, out in enumerate(outs):
        for d in range(4):
            out[d * share : (d + 1) * share, :] = gb[pl.ds(row_of("item", share, 4 * e + d), share), :]
        out[4 * share : used, :] = mine_ref[:more, :] + core_ref[:more, :]
        if out.shape[0] > used:
            out[used:, :] = jnp.zeros((out.shape[0] - used, out.shape[1]), F32)


def pack_call(gbt, mine, core, used, rows):
    rank, n_stores = gbt.shape
    return pl.pallas_call(
        functools.partial(pack_kernel, used),
        out_shape=[jax.ShapeDtypeStruct((rows, rank), F32)] * 4,
        in_specs=[VM] * 3,
        out_specs=[VM] * 4,
        scratch_shapes=[pltpu.VMEM((n_stores, rank), F32)],
        compiler_params=pltpu.CompilerParams(vmem_limit_bytes=8 * MIB),
        cost_estimate=pl.CostEstimate(flops=LONG, bytes_accessed=0, transcendentals=0),
    )(gbt, mine, core)


def core_sum_kernel(own_ref, got_ref, *outs):
    rows = outs[0].shape[0]
    for k, out in enumerate(outs):
        part = slice(k * rows, (k + 1) * rows)
        out[...] = own_ref[part, :] + got_ref[part, :]


def sum_after_kernel(*refs):
    refs[-1][...] = tree([ref[...] for ref in refs[:-2]])


def sum_kernel(*refs):
    rows = refs[-1].shape[0]
    refs[-1][...] = tree([ref[:rows, :] for ref in refs[:-1]])


def mid_kernel(rate_a, rate_b, share, x0, z1, z2, z3, oldb_ref, mine, got, olda_ref, newb_ref, out_ref):
    terms = (x0, z1, z2, z3)
    for k in range(4):
        total = tree([t[(k ^ d) * share : ((k ^ d) + 1) * share, :] for d, t in enumerate(terms)])
        part = slice(k * share, (k + 1) * share)
        newb_ref[part, :] = oldb_ref[part, :] - rate_b * total
    n = mine.shape[0]
    half = n // 2
    out_ref[:half, :] = olda_ref[:half, :] - rate_a * (mine[:half, :] + got[half:, :])
    out_ref[half:n, :] = olda_ref[half:, :] - rate_a * (mine[half:, :] + got[:half, :])
    out_ref[n:, :] = tree([t[4 * share :, :] for t in terms])


def deal_kernel(share, q0, r1, r2, r3, *outs):
    for d, out in enumerate(outs):
        part = slice(d * share, (d + 1) * share)
        out[:share, :] = (q0[part, :] + r1[part, :]) + (r2[part, :] + r3[part, :])
        out[share:, :] = (q0[4 * share :, :] + r1[4 * share :, :]) + (r2[4 * share :, :] + r3[4 * share :, :])


def halves_kernel(t0, u1, u2, u3, after_ref, keep_ref, send_ref):
    half = keep_ref.shape[0]
    grad = (t0[...] + u1[...]) + (u2[...] + u3[...])
    keep_ref[...] = grad[:half, :]
    send_ref[...] = grad[half:, :]


def last_kernel(rate_b, d0, z1, z2, z3, b_ref, newb_ref, weeks_ref):
    share = newb_ref.shape[0]
    total = (d0[...] + z1[...]) + (z2[...] + z3[...])
    newb_ref[...] = b_ref[:share, :] - rate_b * total[:share, :]
    weeks_ref[...] = total[share:, :]


def end_kernel(rate_a, rate_c, count, keep, got, old_ref, e0, e1, e2, e3, c_ref, newa_ref, newc_ref, loss_ref):
    newa_ref[...] = old_ref[: keep.shape[0], :] - rate_a * (keep[...] + got[...])
    total = (e0[...] + e1[...]) + (e2[...] + e3[...])
    weeks = c_ref.shape[0]
    newc_ref[...] = c_ref[...] - rate_c * total[:weeks, :]
    for k in range(2):
        loss_ref[k] = jnp.sum(total[weeks + k : weeks + k + 1, :]) / count


def body(sales, launch_week, open_week, item_factors, store_factors, week_factors):
    weeks, n_items, n_stores = sales.shape
    total_items = n_items * lax.axis_size("item")
    total_stores = n_stores * lax.axis_size("store")
    count = total_items * total_stores * weeks
    rate_a = 40.0 / (total_stores * weeks)
    rate_b = 40.0 / (total_items * weeks)
    rate_c = 40.0 / (total_items * total_stores)
    sub, rank = item_factors.shape
    share = store_factors.shape[0]
    pair, quarter = (2 * sub, rank), (4 * share, rank)

    def over(values, axis, partners):
        return [swap(v, axis, d) for v, d in zip(values, partners)]

    other = swap(item_factors, "store", ZHI)
    own, own_b, late = pl.pallas_call(
        prepare_kernel,
        out_shape=[
            jax.ShapeDtypeStruct((sub, rank), F32),
            jax.ShapeDtypeStruct((share, rank), F32),
            jax.ShapeDtypeStruct((n_items, n_stores), jnp.int32),
        ],
        in_specs=[pl.BlockSpec(memory_space=pltpu.HBM)] * 4,
        out_specs=[VM] * 3,
        scratch_shapes=[
            pltpu.VMEM((n_items // rank, rank), jnp.int32),
            pltpu.VMEM((1, n_stores), jnp.int32),
            pltpu.SemaphoreType.DMA((4,)),
        ],
        compiler_params=pltpu.CompilerParams(vmem_limit_bytes=8 * MIB),
    )(*[
        pltpu.with_memory_space_constraint(x, pltpu.HBM)
        for x in (item_factors, store_factors, launch_week.reshape(-1, rank), open_week.reshape(1, -1))
    ])
    near = over([own_b] * 3, "item", ZLOS)
    mine_a, mine_b = small_call(join_kernel, [pair, quarter], own, other, own_b, *near, flops=LONG)
    rows = [mine_a] + over([mine_a] * 3, "store", OUTER)
    quarters = [mine_b] + over([mine_b] * 3, "item", OUTER)
    items, block_b = small_call(assemble_kernel, [(8 * sub, rank), (n_stores, rank)], *rows, *quarters, flops=LONG)
    others = swap(items, "store", CORE)
    old = jnp.zeros((weeks + 8, rank), F32)
    errors, gbt, old, factor_c = step_call(sub, rate_c, False, sales, late, block_b, week_factors, old, items, others)

    (part_c,) = small_call(sum_kernel, [(weeks + 8, rank)], old, swap(old, "store", CORE))
    got_c = swap(part_c, "store", ZHI)
    send, own = items_grad_call(errors, block_b, factor_c, part_c)
    parts = small_call(core_sum_kernel, [pair] * 4, own, swap(send, "store", CORE))
    parts = [parts[0]] + over(parts[1:], "store", OUTER)
    dealt = pack_call(gbt, part_c, got_c, 4 * share + weeks, 2 * sub + weeks)
    dealt = [dealt[0]] + over(dealt[1:], "item", OUTER)
    (part_a,) = small_call(sum_after_kernel, [pair], *parts, dealt[0])
    got_a = swap(part_a, "store", ZHI)
    (part_b,) = small_call(sum_kernel, [(4 * share + weeks, rank)], *dealt)
    near = over([part_b] * 3, "item", ZLOS)
    mine_b, packed = small_call(
        functools.partial(mid_kernel, rate_a, rate_b, share),
        [quarter, (2 * sub + weeks, rank)],
        part_b, *near, mine_b, part_a, got_a, mine_a,
    )
    rows = [packed] + over([packed] * 3, "store", OUTER)
    quarters = [mine_b] + over([mine_b] * 3, "item", OUTER)
    items, block_b = small_call(
        assemble_kernel, [(8 * sub + weeks, rank), (n_stores, rank)], *rows, *quarters
    )
    others = swap(items, "store", CORE)
    errors, gbt, old, factor_c = step_call(sub, rate_c, True, sales, late, block_b, factor_c, old, items, others)

    (part_c,) = small_call(sum_kernel, [(weeks + 8, rank)], old, swap(old, "store", CORE))
    got_c = swap(part_c, "store", ZHI)
    send, own = items_grad_call(errors, block_b, factor_c, part_c)
    parts = small_call(core_sum_kernel, [pair] * 4, own, swap(send, "store", CORE))
    parts = [parts[0]] + over(parts[1:], "store", OUTER)
    dealt = pack_call(gbt, part_c, got_c, 4 * share + weeks + 8, 4 * share + weeks + 8)
    dealt = [dealt[0]] + over(dealt[1:], "item", OUTER)
    keep, send = small_call(halves_kernel, [(sub, rank)] * 2, *parts, dealt[0])
    got_a = swap(send, "store", ZHI)
    near = small_call(functools.partial(deal_kernel, share), [(share + weeks + 8, rank)] * 4, *dealt)
    near = [near[0]] + over(near[1:], "item", ZLOS)
    shard_b, part_c = small_call(
        functools.partial(last_kernel, rate_b), [(share, rank), (weeks + 8, rank)], *near, mine_b
    )
    shard_a, factor_c, losses = pl.pallas_call(
        functools.partial(end_kernel, rate_a, rate_c, 2.0 * count),
        out_shape=[jax.ShapeDtypeStruct(s, F32) for s in ((sub, rank), (weeks, rank), (2,))],
        in_specs=[VM] * 8,
        out_specs=[VM, VM, pl.BlockSpec(memory_space=pltpu.SMEM)],
        compiler_params=pltpu.CompilerParams(vmem_limit_bytes=8 * MIB),
        cost_estimate=pl.CostEstimate(flops=0, bytes_accessed=0, transcendentals=0),
    )(keep, got_a, packed, part_c, *over([part_c] * 3, "store", OUTER), factor_c)
    return shard_a, shard_b, factor_c, losses


def solution(mesh):
    in_specs = (
        P(None, "item", "store"),
        P("item"),
        P("store"),
        P(("item", "store"), None),
        P(("store", "item"), None),
        P(),
    )
    out_specs = (P(("item", "store"), None), P(("store", "item"), None), P(), P())
    return jax.shard_map(body, mesh=mesh, in_specs=in_specs, out_specs=out_specs, check_vma=False)
```

```python
import functools

import jax
import jax.numpy as jnp
from jax import lax
from jax.experimental import pallas as pl
from jax.experimental.pallas import tpu as pltpu
from jax.sharding import PartitionSpec as P

CORE, ZHI = 1, 2
OUTER = (4, 8, 12)
ZLOS = (1, 2, 3)
MIB = 1 << 20
LONG = 10**11
F32 = jnp.float32
BF16 = jnp.bfloat16
VM = pl.BlockSpec(memory_space=pltpu.VMEM)


def swap(value, axis, bits):
    return lax.ppermute(value, axis, [(i, i ^ bits) for i in range(16)])


def chip_swap(value, item_way, store_way):
    pairs = []
    for item in range(16):
        for store in range(16):
            if store & CORE:
                pairs.append((item * 16 + store, (item ^ store_way) * 16 + store))
            elif item_way:
                pairs.append((item * 16 + store, item * 16 + (store ^ item_way)))
    return lax.ppermute(value, ("item", "store"), pairs)


def split(value):
    high = value.astype(BF16)
    return high, (value - high.astype(F32)).astype(BF16)


def row_of(axis, rows, bits):
    return pl.multiple_of((lax.axis_index(axis) ^ bits) * rows, rows)


def tree(values):
    while len(values) > 1:
        values = [a + b for a, b in zip(values[::2], values[1::2])]
    return values[0]


def small_call(kernel, outs, *args, flops=None, scratch=()):
    cost = pl.CostEstimate(flops=flops or 0, bytes_accessed=0, transcendentals=0)
    outs = [o if isinstance(o, jax.ShapeDtypeStruct) else jax.ShapeDtypeStruct(o, F32) for o in outs]
    return pl.pallas_call(
        kernel,
        out_shape=outs,
        in_specs=[VM] * len(args),
        out_specs=[VM] * len(outs),
        scratch_shapes=scratch,
        compiler_params=pltpu.CompilerParams(vmem_limit_bytes=8 * MIB),
        cost_estimate=cost,
    )(*args)


def step_kernel(rate_c, riding, *refs):
    sales_ref, late_ref, a_ref, b_ref, c_ref, old_weeks = refs[:6]
    er, gbt_ref, weeks_ref, newc_ref, a3, at = refs[-6:]
    weeks, n_items, n_stores = sales_ref.shape
    rank = a_ref.shape[1]
    rows = 256

    a = a_ref[...]
    high, low = split(a)
    a3[:, :rank] = high
    a3[:, rank : 2 * rank] = low
    a3[:, 2 * rank :] = high
    high, low = split(a.T)
    at[:rank, :] = high
    at[rank:, :] = low
    b = b_ref[...]
    bt = b.T
    c = c_ref[...]
    if riding:
        c = c - rate_c * refs[6][...]
    newc_ref[...] = c

    def factor(w):
        high, low = split(b * c[w : w + 1, :])
        return jnp.concatenate([high, high, low], axis=1)

    def errors(w, i, bc3, total_s):
        part = slice(i * rows, (i + 1) * rows)
        recon = lax.dot_general(a3[part, :], bc3, (((1,), (1,)), ((), ())), preferred_element_type=F32)
        error = jnp.where(late_ref[part, :] <= w, recon - sales_ref[w, part, :], 0.0)
        er[w, part, :] = error.astype(BF16)
        return total_s + jnp.sum((error * error).reshape(rows // 8, 8, n_stores), axis=0)

    n = n_items // rows
    total_s = jnp.zeros((8, n_stores), F32)
    gbt = jnp.zeros((rank, n_stores), F32)
    week_columns = []
    bc3 = factor(0)
    for i in range(n):
        total_s = errors(0, i, bc3, total_s)
    for w in range(weeks):
        if w + 1 < weeks:
            bc3 = factor(w + 1)
            for i in range(n):
                total_s = errors(w + 1, i, bc3, total_s)
        x = jnp.dot(at[...], er[w], preferred_element_type=F32)
        x = x[:rank, :] + x[rank:, :]
        week_columns.append(jnp.sum(x * bt, axis=1, keepdims=True))
        turn = jnp.broadcast_to(c[w : w + 1, :], (rank, rank)).T
        gbt = gbt + jnp.concatenate([turn] * (n_stores // rank), axis=1) * x

    lane = lax.broadcasted_iota(jnp.int32, (rank, rank), 1)
    gc = jnp.zeros((rank, rank), F32)
    for w in range(weeks):
        gc = jnp.where(lane == w, week_columns[w], gc)
    gc = gc.T[:weeks, :]
    s = jnp.sum(total_s, axis=0, keepdims=True)
    loss = s[:, :rank]
    for i in range(1, n_stores // rank):
        loss = loss + s[:, i * rank : (i + 1) * rank]
    at_row = lax.broadcasted_iota(jnp.int32, (8, rank), 0)
    losses = jnp.where(at_row == int(riding), loss, old_weeks[weeks:, :])
    gbt_ref[...] = gbt
    weeks_ref[:weeks, :] = gc
    weeks_ref[weeks:, :] = losses


def step_call(rate_c, riding, sales, late, block_a, block_b, factor_c, old_weeks, *grad_c):
    weeks, n_items, n_stores = sales.shape
    rank = block_b.shape[1]
    outs = [(rank, n_stores), (weeks + 8, rank), (weeks, rank)]
    args = [sales, late, block_a, block_b, factor_c, old_weeks, *grad_c]
    return pl.pallas_call(
        functools.partial(step_kernel, rate_c, riding),
        out_shape=[jax.ShapeDtypeStruct(sales.shape, BF16)] + [jax.ShapeDtypeStruct(s, F32) for s in outs],
        in_specs=[VM] * len(args),
        out_specs=[VM] * (1 + len(outs)),
        scratch_shapes=[
            pltpu.VMEM((n_items, 3 * rank), BF16),
            pltpu.VMEM((2 * rank, n_items), BF16),
        ],
        compiler_params=pltpu.CompilerParams(vmem_limit_bytes=28 * MIB),
        cost_estimate=pl.CostEstimate(
            flops=4 * n_items * n_stores * weeks * rank, bytes_accessed=4 * n_items * n_stores * weeks, transcendentals=0
        ),
    )(*args)


def items_grad_kernel(er, b_ref, c_ref, after_ref, send_ref, own_ref, ga):
    weeks, n_items, n_stores = er.shape
    rank = b_ref.shape[1]
    rows = 256
    b = b_ref[...]
    factors = [jnp.concatenate(split(b * c_ref[w : w + 1, :]), axis=1) for w in range(weeks)]
    for i in range(n_items // rows):
        part = slice(i * rows, (i + 1) * rows)
        g = jnp.dot(er[0, part, :], factors[0], preferred_element_type=F32)
        for w in range(1, weeks):
            g = g + jnp.dot(er[w, part, :], factors[w], preferred_element_type=F32)
        ga[part, :] = g[:, :rank] + g[:, rank:]
    sub = send_ref.shape[0] // 8
    for other, out in ((0, own_ref), (1, send_ref)):
        for d in range(4):
            for h in range(2):
                row = row_of("store", sub, 4 * d + 2 * h + other)
                out[(d * 2 + h) * sub : (d * 2 + h + 1) * sub, :] = ga[pl.ds(row, sub), :]


def items_grad_call(er, block_b, factor_c, after):
    weeks, n_items, n_stores = er.shape
    rank = block_b.shape[1]
    return pl.pallas_call(
        items_grad_kernel,
        out_shape=[jax.ShapeDtypeStruct((n_items // 2, rank), F32)] * 2,
        in_specs=[VM] * 4,
        out_specs=[VM] * 2,
        scratch_shapes=[pltpu.VMEM((n_items, rank), F32)],
        compiler_params=pltpu.CompilerParams(vmem_limit_bytes=16 * MIB),
        cost_estimate=pl.CostEstimate(flops=0, bytes_accessed=0, transcendentals=0),
    )(er, block_b, factor_c, after)


def prepare_kernel(a_hbm, b_hbm, launch_hbm, open_hbm, own_ref, b_ref, late_ref, launch_ref, open_ref, sems):
    pairs = ((b_hbm, b_ref), (launch_hbm, launch_ref), (open_hbm, open_ref), (a_hbm, own_ref))
    copies = [pltpu.make_async_copy(x, y, sems.at[k]) for k, (x, y) in enumerate(pairs)]
    for copy in copies:
        copy.start()
    for copy in copies:
        copy.wait()
    lanes = launch_ref.shape[1]
    opened = open_ref[...]
    for k in range(launch_ref.shape[0]):
        turned = jnp.broadcast_to(launch_ref[k : k + 1, :], (lanes, lanes)).T
        for j in range(opened.shape[1] // lanes):
            part = slice(j * lanes, (j + 1) * lanes)
            late_ref[k * lanes : (k + 1) * lanes, part] = jnp.maximum(turned, opened[:, part])


def on_core(which):
    return pl.when(lax.axis_index("store") % 2 == which)


def near_kernel(own_a, other_a, own_b, other_b, z1, z2):
    sub, share = own_a.shape[0], own_b.shape[0]

    @on_core(0)
    def _():
        z1[:sub, :] = own_a[...]
        z1[sub:, :] = other_a[...]
        z2[...] = jnp.zeros_like(z2)

    @on_core(1)
    def _():
        z1[...] = jnp.zeros_like(z1)
        for ref in (z1, z2):
            ref[:share, :] = other_b[...]
            ref[share : 2 * share, :] = own_b[...]


def join_kernel(z1, z2, g1, g2, g3, out_ref):
    rows, few = z1.shape[0], z2.shape[0]

    @on_core(0)
    def _():
        out_ref[:rows, :] = z1[...]
        out_ref[rows:, :] = g1[...]

    @on_core(1)
    def _():
        out_ref[:few, :] = z2[...]
        out_ref[few : 2 * few, :] = g1[:few, :]
        out_ref[2 * few : 3 * few, :] = g2[...]
        out_ref[3 * few : 4 * few, :] = g3[...]
        out_ref[4 * few :, :] = jnp.zeros((out_ref.shape[0] - 4 * few, out_ref.shape[1]), F32)


def merge_kernel(sub, share, mine, other, out_ref):
    weeks = mine.shape[0] - 2 * sub - 4 * share
    first = 2 * sub + weeks

    @on_core(0)
    def _():
        for h in range(2):
            part = slice(h * sub, (h + 1) * sub)
            out_ref[2 * h * sub : (2 * h + 1) * sub, :] = mine[part, :]
            out_ref[(2 * h + 1) * sub : (2 * h + 2) * sub, :] = other[part, :]
        out_ref[4 * sub :, :] = mine[2 * sub : first, :]

    @on_core(1)
    def _():
        for d in range(4):
            part = slice(first + d * share, first + (d + 1) * share)
            out_ref[2 * d * share : (2 * d + 1) * share, :] = other[part, :]
            out_ref[(2 * d + 1) * share : (2 * d + 2) * share, :] = mine[part, :]
        out_ref[8 * share :, :] = jnp.zeros((out_ref.shape[0] - 8 * share, out_ref.shape[1]), F32)


def stack_kernel(rows, w0, w1, w2, w3, out_ref):
    for d, ref in enumerate((w0, w1, w2, w3)):
        out_ref[d * rows : (d + 1) * rows, :] = ref[:rows, :]
    if w0.shape[0] > rows:
        out_ref[4 * rows :, :] = (w0[rows:, :] + w1[rows:, :]) + (w2[rows:, :] + w3[rows:, :])


def unstack_kernel(sub, share, mine, other, a_ref, b_ref, near_a, near_b, *weeks_ref):
    core = lax.axis_index("store") % 2
    store, item = lax.axis_index("store") - core, lax.axis_index("item")
    rows = 4 * sub
    for which, items, stores in ((0, mine, other), (1, other, mine)):

        @on_core(which)
        def _():
            for d in range(4):
                for h in range(2):
                    for o in range(2):
                        to = pl.multiple_of(((store ^ (4 * d + 2 * h)) + o) * sub, sub)
                        at = d * rows + (2 * h + o) * sub
                        a_ref[pl.ds(to, sub), :] = items[at : at + sub, :]
            for e in range(4):
                for d in range(4):
                    to = pl.multiple_of((item ^ (4 * e + d)) * share, share)
                    at = e * rows + (2 * d + which) * share
                    b_ref[pl.ds(to, share), :] = stores[at : at + share, :]
            for h in range(2):
                at = (2 * h + which) * sub
                near_a[h * sub : (h + 1) * sub, :] = items[at : at + sub, :]
            for d in range(4):
                at = (2 * d + which) * share
                near_b[d * share : (d + 1) * share, :] = stores[at : at + share, :]
            for ref in weeks_ref:
                ref[...] = items[4 * rows :, :]


def far_gather(sub, share, value, weeks, flops=None):
    rank = value.shape[1]
    rows = [value] + [chip_swap(value, d, d) for d in OUTER]
    (stack,) = small_call(
        functools.partial(stack_kernel, 4 * sub), [(16 * sub + weeks, rank)], *rows, flops=flops
    )
    outs = [(16 * sub, rank), (16 * share, rank), (2 * sub, rank), (4 * share, rank)]
    outs = outs + ([(weeks, rank)] if weeks else [])
    other = swap(stack, "store", CORE)
    return small_call(functools.partial(unstack_kernel, sub, share), outs, stack, other)


def pack_kernel(used, gbt_ref, mine_ref, core_ref, *refs):
    outs, gb = refs[:4], refs[4]
    gb[...] = gbt_ref[...].T
    share = gb.shape[0] // 16
    more = used - 4 * share
    for e, out in enumerate(outs):
        for d in range(4):
            out[d * share : (d + 1) * share, :] = gb[pl.ds(row_of("item", share, 4 * e + d), share), :]
        out[4 * share : used, :] = mine_ref[:more, :] + core_ref[:more, :]
        if out.shape[0] > used:
            out[used:, :] = jnp.zeros((out.shape[0] - used, out.shape[1]), F32)


def pack_call(gbt, mine, core, used, rows):
    rank, n_stores = gbt.shape
    return pl.pallas_call(
        functools.partial(pack_kernel, used),
        out_shape=[jax.ShapeDtypeStruct((rows, rank), F32)] * 4,
        in_specs=[VM] * 3,
        out_specs=[VM] * 4,
        scratch_shapes=[pltpu.VMEM((n_stores, rank), F32)],
        compiler_params=pltpu.CompilerParams(vmem_limit_bytes=8 * MIB),
        cost_estimate=pl.CostEstimate(flops=LONG, bytes_accessed=0, transcendentals=0),
    )(gbt, mine, core)


def core_sum_kernel(own_ref, got_ref, *outs):
    rows = outs[0].shape[0]
    for k, out in enumerate(outs):
        part = slice(k * rows, (k + 1) * rows)
        out[...] = own_ref[part, :] + got_ref[part, :]


def sum_after_kernel(*refs):
    refs[-1][...] = tree([ref[...] for ref in refs[:-2]])


def sum_kernel(*refs):
    rows = refs[-1].shape[0]
    refs[-1][...] = tree([ref[:rows, :] for ref in refs[:-1]])


def mid_kernel(rate_a, rate_b, share, x0, z1, z2, z3, oldb_ref, mine, got, olda_ref, out_ref):
    terms = (x0, z1, z2, z3)
    n = mine.shape[0]
    half = n // 2
    first = n + x0.shape[0] - 4 * share
    for k in range(4):
        total = tree([t[(k ^ d) * share : ((k ^ d) + 1) * share, :] for d, t in enumerate(terms)])
        part = slice(k * share, (k + 1) * share)
        out_ref[first + k * share : first + (k + 1) * share, :] = oldb_ref[part, :] - rate_b * total
    out_ref[:half, :] = olda_ref[:half, :] - rate_a * (mine[:half, :] + got[half:, :])
    out_ref[half:n, :] = olda_ref[half:, :] - rate_a * (mine[half:, :] + got[:half, :])
    out_ref[n:first, :] = tree([t[4 * share :, :] for t in terms])


def deal_kernel(share, q0, r1, r2, r3, *outs):
    for d, out in enumerate(outs):
        part = slice(d * share, (d + 1) * share)
        out[:share, :] = (q0[part, :] + r1[part, :]) + (r2[part, :] + r3[part, :])
        out[share:, :] = (q0[4 * share :, :] + r1[4 * share :, :]) + (r2[4 * share :, :] + r3[4 * share :, :])


def halves_kernel(t0, u1, u2, u3, after_ref, keep_ref, send_ref):
    half = keep_ref.shape[0]
    grad = (t0[...] + u1[...]) + (u2[...] + u3[...])
    keep_ref[...] = grad[:half, :]
    send_ref[...] = grad[half:, :]


def last_kernel(rate_b, d0, z1, z2, z3, b_ref, newb_ref, weeks_ref):
    share = newb_ref.shape[0]
    total = (d0[...] + z1[...]) + (z2[...] + z3[...])
    newb_ref[...] = b_ref[:share, :] - rate_b * total[:share, :]
    weeks_ref[...] = total[share:, :]


def end_kernel(rate_a, rate_c, count, keep, got, old_ref, e0, e1, e2, e3, c_ref, newa_ref, newc_ref, loss_ref):
    newa_ref[...] = old_ref[: keep.shape[0], :] - rate_a * (keep[...] + got[...])
    total = (e0[...] + e1[...]) + (e2[...] + e3[...])
    weeks = c_ref.shape[0]
    newc_ref[...] = c_ref[...] - rate_c * total[:weeks, :]
    for k in range(2):
        loss_ref[k] = jnp.sum(total[weeks + k : weeks + k + 1, :]) / count


def body(sales, launch_week, open_week, item_factors, store_factors, week_factors):
    weeks, n_items, n_stores = sales.shape
    total_items = n_items * lax.axis_size("item")
    total_stores = n_stores * lax.axis_size("store")
    count = total_items * total_stores * weeks
    rate_a = 40.0 / (total_stores * weeks)
    rate_b = 40.0 / (total_items * weeks)
    rate_c = 40.0 / (total_items * total_stores)
    sub, rank = item_factors.shape
    share = store_factors.shape[0]
    pair, quarter = (2 * sub, rank), (4 * share, rank)

    def over(values, axis, partners):
        return [swap(v, axis, d) for v, d in zip(values, partners)]

    other_a = swap(item_factors, "store", CORE)
    other_b = swap(store_factors, "store", CORE)
    own, own_b, late = pl.pallas_call(
        prepare_kernel,
        out_shape=[
            jax.ShapeDtypeStruct((sub, rank), F32),
            jax.ShapeDtypeStruct((share, rank), F32),
            jax.ShapeDtypeStruct((n_items, n_stores), jnp.int32),
        ],
        in_specs=[pl.BlockSpec(memory_space=pltpu.HBM)] * 4,
        out_specs=[VM] * 3,
        scratch_shapes=[
            pltpu.VMEM((n_items // rank, rank), jnp.int32),
            pltpu.VMEM((1, n_stores), jnp.int32),
            pltpu.SemaphoreType.DMA((4,)),
        ],
        compiler_params=pltpu.CompilerParams(vmem_limit_bytes=8 * MIB),
    )(*[
        pltpu.with_memory_space_constraint(x, pltpu.HBM)
        for x in (item_factors, store_factors, launch_week.reshape(-1, rank), open_week.reshape(1, -1))
    ])
    z1, z2 = small_call(near_kernel, [pair, (2 * share, rank)], own, other_a, own_b, other_b)
    near = [chip_swap(z1, ZHI, 1), chip_swap(z2, 0, 2), chip_swap(z2, 0, 3)]
    (value,) = small_call(join_kernel, [(4 * sub, rank)], z1, z2, *near)
    block_a, block_b, mine_a, mine_b = far_gather(sub, share, value, 0, flops=LONG)
    old = jnp.zeros((weeks + 8, rank), F32)
    errors, gbt, old, factor_c = step_call(rate_c, False, sales, late, block_a, block_b, week_factors, old)

    (part_c,) = small_call(sum_kernel, [(weeks + 8, rank)], old, swap(old, "store", CORE))
    got_c = swap(part_c, "store", ZHI)
    send, own = items_grad_call(errors, block_b, factor_c, part_c)
    parts = small_call(core_sum_kernel, [pair] * 4, own, swap(send, "store", CORE))
    parts = [parts[0]] + over(parts[1:], "store", OUTER)
    dealt = pack_call(gbt, part_c, got_c, 4 * share + weeks, 2 * sub + weeks)
    dealt = [dealt[0]] + over(dealt[1:], "item", OUTER)
    (part_a,) = small_call(sum_after_kernel, [pair], *parts, dealt[0])
    got_a = swap(part_a, "store", ZHI)
    (part_b,) = small_call(sum_kernel, [(4 * share + weeks, rank)], *dealt)
    near = over([part_b] * 3, "item", ZLOS)
    (new,) = small_call(
        functools.partial(mid_kernel, rate_a, rate_b, share),
        [(2 * sub + weeks + 4 * share, rank)],
        part_b, *near, mine_b, part_a, got_a, mine_a,
    )
    (value,) = small_call(
        functools.partial(merge_kernel, sub, share), [(4 * sub + weeks, rank)], new, swap(new, "store", CORE)
    )
    block_a, block_b, mine_a, mine_b, grad_c = far_gather(sub, share, value, weeks)
    errors, gbt, old, factor_c = step_call(rate_c, True, sales, late, block_a, block_b, factor_c, old, grad_c)

    (part_c,) = small_call(sum_kernel, [(weeks + 8, rank)], old, swap(old, "store", CORE))
    got_c = swap(part_c, "store", ZHI)
    send, own = items_grad_call(errors, block_b, factor_c, part_c)
    parts = small_call(core_sum_kernel, [pair] * 4, own, swap(send, "store", CORE))
    parts = [parts[0]] + over(parts[1:], "store", OUTER)
    dealt = pack_call(gbt, part_c, got_c, 4 * share + weeks + 8, 4 * share + weeks + 8)
    dealt = [dealt[0]] + over(dealt[1:], "item", OUTER)
    keep, send = small_call(halves_kernel, [(sub, rank)] * 2, *parts, dealt[0])
    got_a = swap(send, "store", ZHI)
    near = small_call(functools.partial(deal_kernel, share), [(share + weeks + 8, rank)] * 4, *dealt)
    near = [near[0]] + over(near[1:], "item", ZLOS)
    shard_b, part_c = small_call(
        functools.partial(last_kernel, rate_b), [(share, rank), (weeks + 8, rank)], *near, mine_b
    )
    shard_a, factor_c, losses = pl.pallas_call(
        functools.partial(end_kernel, rate_a, rate_c, 2.0 * count),
        out_shape=[jax.ShapeDtypeStruct(s, F32) for s in ((sub, rank), (weeks, rank), (2,))],
        in_specs=[VM] * 8,
        out_specs=[VM, VM, pl.BlockSpec(memory_space=pltpu.SMEM)],
        compiler_params=pltpu.CompilerParams(vmem_limit_bytes=8 * MIB),
        cost_estimate=pl.CostEstimate(flops=0, bytes_accessed=0, transcendentals=0),
    )(keep, got_a, mine_a, part_c, *over([part_c] * 3, "store", OUTER), factor_c)
    return shard_a, shard_b, factor_c, losses


def solution(mesh):
    in_specs = (
        P(None, "item", "store"),
        P("item"),
        P("store"),
        P(("item", "store"), None),
        P(("store", "item"), None),
        P(),
    )
    out_specs = (P(("item", "store"), None), P(("store", "item"), None), P(), P())
    return jax.shard_map(body, mesh=mesh, in_specs=in_specs, out_specs=out_specs, check_vma=False)
```

```python
import functools

import jax
import jax.numpy as jnp
from jax import lax
from jax.experimental import pallas as pl
from jax.experimental.pallas import tpu as pltpu
from jax.sharding import PartitionSpec as P

CORE, ZHI = 1, 2
OUTER = (4, 8, 12)
ZLOS = (1, 2, 3)
MIB = 1 << 20
LONG = 10**11
F32 = jnp.float32
BF16 = jnp.bfloat16
VM = pl.BlockSpec(memory_space=pltpu.VMEM)


def swap(value, axis, bits):
    return lax.ppermute(value, axis, [(i, i ^ bits) for i in range(16)])


def chip_swap(value, item_way, store_way):
    pairs = []
    for item in range(16):
        for store in range(16):
            if store & CORE:
                pairs.append((item * 16 + store, (item ^ store_way) * 16 + store))
            elif item_way:
                pairs.append((item * 16 + store, item * 16 + (store ^ item_way)))
    return lax.ppermute(value, ("item", "store"), pairs)


def split(value):
    high = value.astype(BF16)
    return high, (value - high.astype(F32)).astype(BF16)


def row_of(axis, rows, bits):
    return pl.multiple_of((lax.axis_index(axis) ^ bits) * rows, rows)


def tree(values):
    while len(values) > 1:
        values = [a + b for a, b in zip(values[::2], values[1::2])]
    return values[0]


def small_call(kernel, outs, *args, flops=None, scratch=()):
    cost = pl.CostEstimate(flops=flops or 0, bytes_accessed=0, transcendentals=0)
    outs = [o if isinstance(o, jax.ShapeDtypeStruct) else jax.ShapeDtypeStruct(o, F32) for o in outs]
    return pl.pallas_call(
        kernel,
        out_shape=outs,
        in_specs=[VM] * len(args),
        out_specs=[VM] * len(outs),
        scratch_shapes=scratch,
        compiler_params=pltpu.CompilerParams(vmem_limit_bytes=8 * MIB),
        cost_estimate=cost,
    )(*args)


def step_kernel(rate_c, riding, *refs):
    sales_ref, late_ref, a_ref, b_ref, c_ref, old_weeks = refs[:6]
    er, gbt_ref, weeks_ref, newc_ref, a3, at = refs[-6:]
    weeks, n_items, n_stores = sales_ref.shape
    rank = a_ref.shape[1]
    rows = 256

    a = a_ref[...]
    high, low = split(a)
    a3[:, :rank] = high
    a3[:, rank : 2 * rank] = low
    a3[:, 2 * rank :] = high
    high, low = split(a.T)
    at[:rank, :] = high
    at[rank:, :] = low
    b = b_ref[...]
    bt = b.T
    c = c_ref[...]
    if riding:
        c = c - rate_c * refs[6][...]
    newc_ref[...] = c

    def factor(w):
        high, low = split(b * c[w : w + 1, :])
        return jnp.concatenate([high, high, low], axis=1)

    def errors(w, i, bc3, total_s):
        part = slice(i * rows, (i + 1) * rows)
        recon = lax.dot_general(a3[part, :], bc3, (((1,), (1,)), ((), ())), preferred_element_type=F32)
        error = jnp.where(late_ref[part, :] <= w, recon - sales_ref[w, part, :], 0.0)
        er[w, part, :] = error.astype(BF16)
        return total_s + jnp.sum((error * error).reshape(rows // 8, 8, n_stores), axis=0)

    n = n_items // rows
    total_s = jnp.zeros((8, n_stores), F32)
    gbt = jnp.zeros((rank, n_stores), F32)
    week_columns = []
    bc3 = factor(0)
    for i in range(n):
        total_s = errors(0, i, bc3, total_s)
    for w in range(weeks):
        if w + 1 < weeks:
            bc3 = factor(w + 1)
            for i in range(n):
                total_s = errors(w + 1, i, bc3, total_s)
        x = jnp.dot(at[...], er[w], preferred_element_type=F32)
        x = x[:rank, :] + x[rank:, :]
        week_columns.append(jnp.sum(x * bt, axis=1, keepdims=True))
        turn = jnp.broadcast_to(c[w : w + 1, :], (rank, rank)).T
        gbt = gbt + jnp.concatenate([turn] * (n_stores // rank), axis=1) * x

    lane = lax.broadcasted_iota(jnp.int32, (rank, rank), 1)
    gc = jnp.zeros((rank, rank), F32)
    for w in range(weeks):
        gc = jnp.where(lane == w, week_columns[w], gc)
    gc = gc.T[:weeks, :]
    s = jnp.sum(total_s, axis=0, keepdims=True)
    loss = s[:, :rank]
    for i in range(1, n_stores // rank):
        loss = loss + s[:, i * rank : (i + 1) * rank]
    at_row = lax.broadcasted_iota(jnp.int32, (8, rank), 0)
    losses = jnp.where(at_row == int(riding), loss, old_weeks[weeks:, :])
    gbt_ref[...] = gbt
    weeks_ref[:weeks, :] = gc
    weeks_ref[weeks:, :] = losses


def step_call(rate_c, riding, sales, late, block_a, block_b, factor_c, old_weeks, *grad_c):
    weeks, n_items, n_stores = sales.shape
    rank = block_b.shape[1]
    outs = [(rank, n_stores), (weeks + 8, rank), (weeks, rank)]
    args = [sales, late, block_a, block_b, factor_c, old_weeks, *grad_c]
    return pl.pallas_call(
        functools.partial(step_kernel, rate_c, riding),
        out_shape=[jax.ShapeDtypeStruct(sales.shape, BF16)] + [jax.ShapeDtypeStruct(s, F32) for s in outs],
        in_specs=[VM] * len(args),
        out_specs=[VM] * (1 + len(outs)),
        scratch_shapes=[
            pltpu.VMEM((n_items, 3 * rank), BF16),
            pltpu.VMEM((2 * rank, n_items), BF16),
        ],
        compiler_params=pltpu.CompilerParams(vmem_limit_bytes=28 * MIB),
        cost_estimate=pl.CostEstimate(
            flops=4 * n_items * n_stores * weeks * rank, bytes_accessed=4 * n_items * n_stores * weeks, transcendentals=0
        ),
    )(*args)


def items_grad_kernel(er, b_ref, c_ref, after_ref, send_ref, own_ref, ga):
    weeks, n_items, n_stores = er.shape
    rank = b_ref.shape[1]
    rows = 256
    b = b_ref[...]
    factors = [jnp.concatenate(split(b * c_ref[w : w + 1, :]), axis=1) for w in range(weeks)]
    for i in range(n_items // rows):
        part = slice(i * rows, (i + 1) * rows)
        g = jnp.dot(er[0, part, :], factors[0], preferred_element_type=F32)
        for w in range(1, weeks):
            g = g + jnp.dot(er[w, part, :], factors[w], preferred_element_type=F32)
        ga[part, :] = g[:, :rank] + g[:, rank:]
    sub = send_ref.shape[0] // 8
    for other, out in ((0, own_ref), (1, send_ref)):
        for d in range(4):
            for h in range(2):
                row = row_of("store", sub, 4 * d + 2 * h + other)
                out[(d * 2 + h) * sub : (d * 2 + h + 1) * sub, :] = ga[pl.ds(row, sub), :]


def items_grad_call(er, block_b, factor_c, after):
    weeks, n_items, n_stores = er.shape
    rank = block_b.shape[1]
    return pl.pallas_call(
        items_grad_kernel,
        out_shape=[jax.ShapeDtypeStruct((n_items // 2, rank), F32)] * 2,
        in_specs=[VM] * 4,
        out_specs=[VM] * 2,
        scratch_shapes=[pltpu.VMEM((n_items, rank), F32)],
        compiler_params=pltpu.CompilerParams(vmem_limit_bytes=16 * MIB),
        cost_estimate=pl.CostEstimate(flops=0, bytes_accessed=0, transcendentals=0),
    )(er, block_b, factor_c, after)


def prepare_kernel(a_hbm, b_hbm, launch_hbm, open_hbm, own_ref, b_ref, late_ref, launch_ref, open_ref, sems):
    pairs = ((b_hbm, b_ref), (launch_hbm, launch_ref), (open_hbm, open_ref), (a_hbm, own_ref))
    copies = [pltpu.make_async_copy(x, y, sems.at[k]) for k, (x, y) in enumerate(pairs)]
    for copy in copies:
        copy.start()
    for copy in copies:
        copy.wait()
    lanes = launch_ref.shape[1]
    opened = open_ref[...]
    for k in range(launch_ref.shape[0]):
        turned = jnp.broadcast_to(launch_ref[k : k + 1, :], (lanes, lanes)).T
        for j in range(opened.shape[1] // lanes):
            part = slice(j * lanes, (j + 1) * lanes)
            late_ref[k * lanes : (k + 1) * lanes, part] = jnp.maximum(turned, opened[:, part])


def on_core(which):
    return pl.when(lax.axis_index("store") % 2 == which)


def near_kernel(own_a, other_a, own_b, other_b, z1, z2):
    sub, share = own_a.shape[0], own_b.shape[0]

    @on_core(0)
    def _():
        z1[:sub, :] = own_a[...]
        z1[sub:, :] = other_a[...]
        z2[...] = jnp.zeros_like(z2)

    @on_core(1)
    def _():
        z1[...] = jnp.zeros_like(z1)
        for ref in (z1, z2):
            ref[:share, :] = other_b[...]
            ref[share : 2 * share, :] = own_b[...]


def join_kernel(z1, z2, g1, g2, g3, out_ref):
    rows, few = z1.shape[0], z2.shape[0]

    @on_core(0)
    def _():
        out_ref[:rows, :] = z1[...]
        out_ref[rows:, :] = g1[...]

    @on_core(1)
    def _():
        out_ref[:few, :] = z2[...]
        out_ref[few : 2 * few, :] = g1[:few, :]
        out_ref[2 * few : 3 * few, :] = g2[...]
        out_ref[3 * few : 4 * few, :] = g3[...]
        out_ref[4 * few :, :] = jnp.zeros((out_ref.shape[0] - 4 * few, out_ref.shape[1]), F32)


def merge_kernel(sub, share, mine, other, out_ref):
    weeks = mine.shape[0] - 2 * sub - 4 * share
    first = 2 * sub + weeks

    @on_core(0)
    def _():
        for h in range(2):
            part = slice(h * sub, (h + 1) * sub)
            out_ref[2 * h * sub : (2 * h + 1) * sub, :] = mine[part, :]
            out_ref[(2 * h + 1) * sub : (2 * h + 2) * sub, :] = other[part, :]
        out_ref[4 * sub :, :] = mine[2 * sub : first, :]

    @on_core(1)
    def _():
        for d in range(4):
            part = slice(first + d * share, first + (d + 1) * share)
            out_ref[2 * d * share : (2 * d + 1) * share, :] = other[part, :]
            out_ref[(2 * d + 1) * share : (2 * d + 2) * share, :] = mine[part, :]
        out_ref[8 * share :, :] = jnp.zeros((out_ref.shape[0] - 8 * share, out_ref.shape[1]), F32)


def unstack_kernel(sub, share, *refs):
    mine, other, (a_ref, b_ref, near_a, near_b), weeks_ref = refs[:4], refs[4:8], refs[8:12], refs[12:]
    core = lax.axis_index("store") % 2
    store, item = lax.axis_index("store") - core, lax.axis_index("item")
    rows = 4 * sub
    for which, items, stores in ((0, mine, other), (1, other, mine)):

        @on_core(which)
        def _():
            for d in range(4):
                for h in range(2):
                    for o in range(2):
                        to = pl.multiple_of(((store ^ (4 * d + 2 * h)) + o) * sub, sub)
                        at = (2 * h + o) * sub
                        a_ref[pl.ds(to, sub), :] = items[d][at : at + sub, :]
            for e in range(4):
                for d in range(4):
                    to = pl.multiple_of((item ^ (4 * e + d)) * share, share)
                    at = (2 * d + which) * share
                    b_ref[pl.ds(to, share), :] = stores[e][at : at + share, :]
            for h in range(2):
                at = (2 * h + which) * sub
                near_a[h * sub : (h + 1) * sub, :] = items[0][at : at + sub, :]
            for d in range(4):
                at = (2 * d + which) * share
                near_b[d * share : (d + 1) * share, :] = stores[0][at : at + share, :]
            for ref in weeks_ref:
                ref[...] = tree([item[rows:, :] for item in items])


def far_gather(sub, share, value, weeks):
    rank = value.shape[1]
    rows = [value] + [chip_swap(value, d, d) for d in OUTER]
    outs = [(16 * sub, rank), (16 * share, rank), (2 * sub, rank), (4 * share, rank)]
    outs = outs + ([(weeks, rank)] if weeks else [])
    others = [swap(row, "store", CORE) for row in rows]
    return small_call(functools.partial(unstack_kernel, sub, share), outs, *rows, *others)


def pack_kernel(used, gbt_ref, mine_ref, core_ref, *refs):
    outs, gb = refs[:4], refs[4]
    gb[...] = gbt_ref[...].T
    share = gb.shape[0] // 16
    more = used - 4 * share
    for e, out in enumerate(outs):
        for d in range(4):
            out[d * share : (d + 1) * share, :] = gb[pl.ds(row_of("item", share, 4 * e + d), share), :]
        out[4 * share : used, :] = mine_ref[:more, :] + core_ref[:more, :]
        if out.shape[0] > used:
            out[used:, :] = jnp.zeros((out.shape[0] - used, out.shape[1]), F32)


def pack_call(gbt, mine, core, used, rows):
    rank, n_stores = gbt.shape
    return pl.pallas_call(
        functools.partial(pack_kernel, used),
        out_shape=[jax.ShapeDtypeStruct((rows, rank), F32)] * 4,
        in_specs=[VM] * 3,
        out_specs=[VM] * 4,
        scratch_shapes=[pltpu.VMEM((n_stores, rank), F32)],
        compiler_params=pltpu.CompilerParams(vmem_limit_bytes=8 * MIB),
        cost_estimate=pl.CostEstimate(flops=LONG, bytes_accessed=0, transcendentals=0),
    )(gbt, mine, core)


def core_sum_kernel(own_ref, got_ref, *outs):
    rows = outs[0].shape[0]
    for k, out in enumerate(outs):
        part = slice(k * rows, (k + 1) * rows)
        out[...] = own_ref[part, :] + got_ref[part, :]


def sum_after_kernel(*refs):
    refs[-1][...] = tree([ref[...] for ref in refs[:-2]])


def sum_kernel(*refs):
    rows = refs[-1].shape[0]
    refs[-1][...] = tree([ref[:rows, :] for ref in refs[:-1]])


def mid_kernel(rate_a, rate_b, share, x0, z1, z2, z3, oldb_ref, mine, got, olda_ref, out_ref):
    terms = (x0, z1, z2, z3)
    n = mine.shape[0]
    half = n // 2
    first = n + x0.shape[0] - 4 * share
    for k in range(4):
        total = tree([t[(k ^ d) * share : ((k ^ d) + 1) * share, :] for d, t in enumerate(terms)])
        part = slice(k * share, (k + 1) * share)
        out_ref[first + k * share : first + (k + 1) * share, :] = oldb_ref[part, :] - rate_b * total
    out_ref[:half, :] = olda_ref[:half, :] - rate_a * (mine[:half, :] + got[half:, :])
    out_ref[half:n, :] = olda_ref[half:, :] - rate_a * (mine[half:, :] + got[:half, :])
    out_ref[n:first, :] = tree([t[4 * share :, :] for t in terms])


def deal_kernel(share, q0, r1, r2, r3, *outs):
    for d, out in enumerate(outs):
        part = slice(d * share, (d + 1) * share)
        out[:share, :] = (q0[part, :] + r1[part, :]) + (r2[part, :] + r3[part, :])
        out[share:, :] = (q0[4 * share :, :] + r1[4 * share :, :]) + (r2[4 * share :, :] + r3[4 * share :, :])


def halves_kernel(t0, u1, u2, u3, after_ref, keep_ref, send_ref):
    half = keep_ref.shape[0]
    grad = (t0[...] + u1[...]) + (u2[...] + u3[...])
    keep_ref[...] = grad[:half, :]
    send_ref[...] = grad[half:, :]


def last_kernel(d0, z1, z2, z3, grad_ref, weeks_ref):
    share = grad_ref.shape[0]
    total = (d0[...] + z1[...]) + (z2[...] + z3[...])
    grad_ref[...] = total[:share, :]
    weeks_ref[...] = total[share:, :]


def end_kernel(rate_a, rate_b, rate_c, count, *refs):
    keep, got, old_ref, e0, e1, e2, e3, c_ref, gradb_ref, b_ref, newa_ref, newb_ref, newc_ref, loss_ref = refs
    newb_ref[...] = b_ref[: newb_ref.shape[0], :] - rate_b * gradb_ref[...]
    newa_ref[...] = old_ref[: keep.shape[0], :] - rate_a * (keep[...] + got[...])
    total = (e0[...] + e1[...]) + (e2[...] + e3[...])
    weeks = c_ref.shape[0]
    newc_ref[...] = c_ref[...] - rate_c * total[:weeks, :]
    for k in range(2):
        loss_ref[k] = jnp.sum(total[weeks + k : weeks + k + 1, :]) / count


def body(sales, launch_week, open_week, item_factors, store_factors, week_factors):
    weeks, n_items, n_stores = sales.shape
    total_items = n_items * lax.axis_size("item")
    total_stores = n_stores * lax.axis_size("store")
    count = total_items * total_stores * weeks
    rate_a = 40.0 / (total_stores * weeks)
    rate_b = 40.0 / (total_items * weeks)
    rate_c = 40.0 / (total_items * total_stores)
    sub, rank = item_factors.shape
    share = store_factors.shape[0]
    pair, quarter = (2 * sub, rank), (4 * share, rank)

    def over(values, axis, partners):
        return [swap(v, axis, d) for v, d in zip(values, partners)]

    other_a = swap(item_factors, "store", CORE)
    other_b = swap(store_factors, "store", CORE)
    own, own_b, late = pl.pallas_call(
        prepare_kernel,
        out_shape=[
            jax.ShapeDtypeStruct((sub, rank), F32),
            jax.ShapeDtypeStruct((share, rank), F32),
            jax.ShapeDtypeStruct((n_items, n_stores), jnp.int32),
        ],
        in_specs=[pl.BlockSpec(memory_space=pltpu.HBM)] * 4,
        out_specs=[VM] * 3,
        scratch_shapes=[
            pltpu.VMEM((n_items // rank, rank), jnp.int32),
            pltpu.VMEM((1, n_stores), jnp.int32),
            pltpu.SemaphoreType.DMA((4,)),
        ],
        compiler_params=pltpu.CompilerParams(vmem_limit_bytes=8 * MIB),
    )(*[
        pltpu.with_memory_space_constraint(x, pltpu.HBM)
        for x in (item_factors, store_factors, launch_week.reshape(-1, rank), open_week.reshape(1, -1))
    ])
    z1, z2 = small_call(near_kernel, [pair, (2 * share, rank)], own, other_a, own_b, other_b)
    near = [chip_swap(z1, ZHI, 1), chip_swap(z2, 0, 2), chip_swap(z2, 0, 3)]
    (value,) = small_call(join_kernel, [(4 * sub, rank)], z1, z2, *near, flops=LONG)
    block_a, block_b, mine_a, mine_b = far_gather(sub, share, value, 0)
    old = jnp.zeros((weeks + 8, rank), F32)
    errors, gbt, old, factor_c = step_call(rate_c, False, sales, late, block_a, block_b, week_factors, old)

    (part_c,) = small_call(sum_kernel, [(weeks + 8, rank)], old, swap(old, "store", CORE))
    got_c = swap(part_c, "store", ZHI)
    send, own = items_grad_call(errors, block_b, factor_c, part_c)
    parts = small_call(core_sum_kernel, [pair] * 4, own, swap(send, "store", CORE))
    parts = [parts[0]] + over(parts[1:], "store", OUTER)
    dealt = pack_call(gbt, part_c, got_c, 4 * share + weeks, 2 * sub + weeks)
    dealt = [dealt[0]] + over(dealt[1:], "item", OUTER)
    (part_a,) = small_call(sum_after_kernel, [pair], *parts, dealt[0])
    got_a = swap(part_a, "store", ZHI)
    (part_b,) = small_call(sum_kernel, [(4 * share + weeks, rank)], *dealt)
    near = over([part_b] * 3, "item", ZLOS)
    (new,) = small_call(
        functools.partial(mid_kernel, rate_a, rate_b, share),
        [(2 * sub + weeks + 4 * share, rank)],
        part_b, *near, mine_b, part_a, got_a, mine_a,
    )
    (value,) = small_call(
        functools.partial(merge_kernel, sub, share), [(4 * sub + weeks, rank)], new, swap(new, "store", CORE)
    )
    block_a, block_b, mine_a, mine_b, grad_c = far_gather(sub, share, value, weeks)
    errors, gbt, old, factor_c = step_call(rate_c, True, sales, late, block_a, block_b, factor_c, old, grad_c)

    (part_c,) = small_call(sum_kernel, [(weeks + 8, rank)], old, swap(old, "store", CORE))
    got_c = swap(part_c, "store", ZHI)
    send, own = items_grad_call(errors, block_b, factor_c, part_c)
    parts = small_call(core_sum_kernel, [pair] * 4, own, swap(send, "store", CORE))
    parts = [parts[0]] + over(parts[1:], "store", OUTER)
    dealt = pack_call(gbt, part_c, got_c, 4 * share + weeks + 8, 4 * share + weeks + 8)
    dealt = [dealt[0]] + over(dealt[1:], "item", OUTER)
    keep, send = small_call(halves_kernel, [(sub, rank)] * 2, *parts, dealt[0])
    got_a = swap(send, "store", ZHI)
    near = small_call(functools.partial(deal_kernel, share), [(share + weeks + 8, rank)] * 4, *dealt)
    near = [near[0]] + over(near[1:], "item", ZLOS)
    grad_b, part_c = small_call(last_kernel, [(share, rank), (weeks + 8, rank)], *near)
    shard_a, shard_b, factor_c, losses = pl.pallas_call(
        functools.partial(end_kernel, rate_a, rate_b, rate_c, 2.0 * count),
        out_shape=[jax.ShapeDtypeStruct(s, F32) for s in ((sub, rank), (share, rank), (weeks, rank), (2,))],
        in_specs=[VM] * 10,
        out_specs=[VM, VM, VM, pl.BlockSpec(memory_space=pltpu.SMEM)],
        compiler_params=pltpu.CompilerParams(vmem_limit_bytes=8 * MIB),
        cost_estimate=pl.CostEstimate(flops=0, bytes_accessed=0, transcendentals=0),
    )(keep, got_a, mine_a, part_c, *over([part_c] * 3, "store", OUTER), factor_c, grad_b, mine_b)
    return shard_a, shard_b, factor_c, losses


def solution(mesh):
    in_specs = (
        P(None, "item", "store"),
        P("item"),
        P("store"),
        P(("item", "store"), None),
        P(("store", "item"), None),
        P(),
    )
    out_specs = (P(("item", "store"), None), P(("store", "item"), None), P(), P())
    return jax.shard_map(body, mesh=mesh, in_specs=in_specs, out_specs=out_specs, check_vma=False)
```

```python
import functools

import jax
import jax.numpy as jnp
from jax import lax
from jax.experimental import pallas as pl
from jax.experimental.pallas import tpu as pltpu
from jax.sharding import PartitionSpec as P

CORE, ZHI = 1, 2
OUTER = (4, 8, 12)
ZLOS = (1, 2, 3)
MIB = 1 << 20
LONG = 10**11
F32 = jnp.float32
BF16 = jnp.bfloat16
VM = pl.BlockSpec(memory_space=pltpu.VMEM)


def swap(value, axis, bits):
    return lax.ppermute(value, axis, [(i, i ^ bits) for i in range(16)])


def chip_swap(value, item_way, store_way):
    pairs = []
    for item in range(16):
        for store in range(16):
            if store & CORE:
                pairs.append((item * 16 + store, (item ^ store_way) * 16 + store))
            elif item_way:
                pairs.append((item * 16 + store, item * 16 + (store ^ item_way)))
    return lax.ppermute(value, ("item", "store"), pairs)


def split(value):
    high = value.astype(BF16)
    return high, (value - high.astype(F32)).astype(BF16)


def row_of(axis, rows, bits):
    return pl.multiple_of((lax.axis_index(axis) ^ bits) * rows, rows)


def tree(values):
    while len(values) > 1:
        values = [a + b for a, b in zip(values[::2], values[1::2])]
    return values[0]


def small_call(kernel, outs, *args, flops=None, scratch=()):
    cost = pl.CostEstimate(flops=flops or 0, bytes_accessed=0, transcendentals=0)
    outs = [o if isinstance(o, jax.ShapeDtypeStruct) else jax.ShapeDtypeStruct(o, F32) for o in outs]
    return pl.pallas_call(
        kernel,
        out_shape=outs,
        in_specs=[VM] * len(args),
        out_specs=[VM] * len(outs),
        scratch_shapes=scratch,
        compiler_params=pltpu.CompilerParams(vmem_limit_bytes=8 * MIB),
        cost_estimate=cost,
    )(*args)


def step_kernel(rate_c, riding, *refs):
    sales_ref, late_ref, a_ref, b_ref, c_ref, old_weeks = refs[:6]
    er, gbt_ref, weeks_ref, newc_ref, a3, at = refs[-6:]
    weeks, n_items, n_stores = sales_ref.shape
    rank = a_ref.shape[1]
    rows = 256

    a = a_ref[...]
    high, low = split(a)
    a3[:, :rank] = high
    a3[:, rank : 2 * rank] = low
    a3[:, 2 * rank :] = high
    high, low = split(a.T)
    at[:rank, :] = high
    at[rank:, :] = low
    b = b_ref[...]
    bt = b.T
    c = c_ref[...]
    if riding:
        c = c - rate_c * refs[6][...]
    newc_ref[...] = c

    def factor(w):
        high, low = split(b * c[w : w + 1, :])
        return jnp.concatenate([high, high, low], axis=1)

    def errors(w, i, bc3, total_s):
        part = slice(i * rows, (i + 1) * rows)
        recon = lax.dot_general(a3[part, :], bc3, (((1,), (1,)), ((), ())), preferred_element_type=F32)
        error = jnp.where(late_ref[part, :] <= w, recon - sales_ref[w, part, :], 0.0)
        er[w, part, :] = error.astype(BF16)
        return total_s + jnp.sum((error * error).reshape(rows // 8, 8, n_stores), axis=0)

    n = n_items // rows
    total_s = jnp.zeros((8, n_stores), F32)
    gbt = jnp.zeros((rank, n_stores), F32)
    week_columns = []
    bc3 = factor(0)
    for i in range(n):
        total_s = errors(0, i, bc3, total_s)
    for w in range(weeks):
        if w + 1 < weeks:
            bc3 = factor(w + 1)
            for i in range(n):
                total_s = errors(w + 1, i, bc3, total_s)
        x = jnp.dot(at[...], er[w], preferred_element_type=F32)
        x = x[:rank, :] + x[rank:, :]
        week_columns.append(jnp.sum(x * bt, axis=1, keepdims=True))
        turn = jnp.broadcast_to(c[w : w + 1, :], (rank, rank)).T
        gbt = gbt + jnp.concatenate([turn] * (n_stores // rank), axis=1) * x

    lane = lax.broadcasted_iota(jnp.int32, (rank, rank), 1)
    gc = jnp.zeros((rank, rank), F32)
    for w in range(weeks):
        gc = jnp.where(lane == w, week_columns[w], gc)
    gc = gc.T[:weeks, :]
    s = jnp.sum(total_s, axis=0, keepdims=True)
    loss = s[:, :rank]
    for i in range(1, n_stores // rank):
        loss = loss + s[:, i * rank : (i + 1) * rank]
    at_row = lax.broadcasted_iota(jnp.int32, (8, rank), 0)
    losses = jnp.where(at_row == int(riding), loss, old_weeks[weeks:, :])
    gbt_ref[...] = gbt
    weeks_ref[:weeks, :] = gc
    weeks_ref[weeks:, :] = losses


def step_call(rate_c, riding, sales, late, block_a, block_b, factor_c, old_weeks, *grad_c):
    weeks, n_items, n_stores = sales.shape
    rank = block_b.shape[1]
    outs = [(rank, n_stores), (weeks + 8, rank), (weeks, rank)]
    args = [sales, late, block_a, block_b, factor_c, old_weeks, *grad_c]
    return pl.pallas_call(
        functools.partial(step_kernel, rate_c, riding),
        out_shape=[jax.ShapeDtypeStruct(sales.shape, BF16)] + [jax.ShapeDtypeStruct(s, F32) for s in outs],
        in_specs=[VM] * len(args),
        out_specs=[VM] * (1 + len(outs)),
        scratch_shapes=[
            pltpu.VMEM((n_items, 3 * rank), BF16),
            pltpu.VMEM((2 * rank, n_items), BF16),
        ],
        compiler_params=pltpu.CompilerParams(vmem_limit_bytes=28 * MIB),
        cost_estimate=pl.CostEstimate(
            flops=4 * n_items * n_stores * weeks * rank, bytes_accessed=4 * n_items * n_stores * weeks, transcendentals=0
        ),
    )(*args)


def items_grad_kernel(er, b_ref, c_ref, after_ref, send_ref, own_ref, ga):
    weeks, n_items, n_stores = er.shape
    rank = b_ref.shape[1]
    rows = 256
    b = b_ref[...]
    factors = [jnp.concatenate(split(b * c_ref[w : w + 1, :]), axis=1) for w in range(weeks)]
    for i in range(n_items // rows):
        part = slice(i * rows, (i + 1) * rows)
        g = jnp.dot(er[0, part, :], factors[0], preferred_element_type=F32)
        for w in range(1, weeks):
            g = g + jnp.dot(er[w, part, :], factors[w], preferred_element_type=F32)
        ga[part, :] = g[:, :rank] + g[:, rank:]
    sub = send_ref.shape[0] // 8
    for other, out in ((0, own_ref), (1, send_ref)):
        for d in range(4):
            for h in range(2):
                row = row_of("store", sub, 4 * d + 2 * h + other)
                out[(d * 2 + h) * sub : (d * 2 + h + 1) * sub, :] = ga[pl.ds(row, sub), :]


def items_grad_call(er, block_b, factor_c, after):
    weeks, n_items, n_stores = er.shape
    rank = block_b.shape[1]
    return pl.pallas_call(
        items_grad_kernel,
        out_shape=[jax.ShapeDtypeStruct((n_items // 2, rank), F32)] * 2,
        in_specs=[VM] * 4,
        out_specs=[VM] * 2,
        scratch_shapes=[pltpu.VMEM((n_items, rank), F32)],
        compiler_params=pltpu.CompilerParams(vmem_limit_bytes=16 * MIB),
        cost_estimate=pl.CostEstimate(flops=0, bytes_accessed=0, transcendentals=0),
    )(er, block_b, factor_c, after)


def prepare_kernel(a_hbm, b_hbm, launch_hbm, open_hbm, own_ref, b_ref, late_ref, launch_ref, open_ref, sems):
    pairs = ((b_hbm, b_ref), (launch_hbm, launch_ref), (open_hbm, open_ref), (a_hbm, own_ref))
    copies = [pltpu.make_async_copy(x, y, sems.at[k]) for k, (x, y) in enumerate(pairs)]
    for copy in copies:
        copy.start()
    for copy in copies:
        copy.wait()
    lanes = launch_ref.shape[1]
    opened = open_ref[...]
    for k in range(launch_ref.shape[0]):
        turned = jnp.broadcast_to(launch_ref[k : k + 1, :], (lanes, lanes)).T
        for j in range(opened.shape[1] // lanes):
            part = slice(j * lanes, (j + 1) * lanes)
            late_ref[k * lanes : (k + 1) * lanes, part] = jnp.maximum(turned, opened[:, part])


def on_core(which):
    return pl.when(lax.axis_index("store") % 2 == which)


def near_kernel(own_a, other_a, own_b, other_b, z1, z2):
    sub, share = own_a.shape[0], own_b.shape[0]

    @on_core(0)
    def _():
        z1[:sub, :] = own_a[...]
        z1[sub:, :] = other_a[...]
        z2[...] = jnp.zeros_like(z2)

    @on_core(1)
    def _():
        z1[...] = jnp.zeros_like(z1)
        for ref in (z1, z2):
            ref[:share, :] = other_b[...]
            ref[share : 2 * share, :] = own_b[...]


def join_kernel(z1, z2, g3, g2, g1, out_ref):
    rows, few = z1.shape[0], z2.shape[0]

    @on_core(0)
    def _():
        out_ref[:rows, :] = z1[...]
        out_ref[rows:, :] = g1[...]

    @on_core(1)
    def _():
        out_ref[:few, :] = z2[...]
        out_ref[few : 2 * few, :] = g1[:few, :]
        out_ref[2 * few : 3 * few, :] = g2[...]
        out_ref[3 * few : 4 * few, :] = g3[...]
        out_ref[4 * few :, :] = jnp.zeros((out_ref.shape[0] - 4 * few, out_ref.shape[1]), F32)


def merge_kernel(sub, share, mine, other, out_ref):
    weeks = mine.shape[0] - 2 * sub - 4 * share
    first = 2 * sub + weeks

    @on_core(0)
    def _():
        for h in range(2):
            part = slice(h * sub, (h + 1) * sub)
            out_ref[2 * h * sub : (2 * h + 1) * sub, :] = mine[part, :]
            out_ref[(2 * h + 1) * sub : (2 * h + 2) * sub, :] = other[part, :]
        out_ref[4 * sub :, :] = mine[2 * sub : first, :] + other[2 * sub : first, :]

    @on_core(1)
    def _():
        for d in range(4):
            part = slice(first + d * share, first + (d + 1) * share)
            out_ref[2 * d * share : (2 * d + 1) * share, :] = other[part, :]
            out_ref[(2 * d + 1) * share : (2 * d + 2) * share, :] = mine[part, :]
        out_ref[8 * share :, :] = jnp.zeros((out_ref.shape[0] - 8 * share, out_ref.shape[1]), F32)


def unstack_kernel(sub, share, *refs):
    mine, other, (a_ref, b_ref, near_a, near_b), weeks_ref = refs[3::-1], refs[7:3:-1], refs[8:12], refs[12:]
    core = lax.axis_index("store") % 2
    store, item = lax.axis_index("store") - core, lax.axis_index("item")
    rows = 4 * sub
    for which, items, stores in ((0, mine, other), (1, other, mine)):

        @on_core(which)
        def _():
            for d in range(4):
                for h in range(2):
                    for o in range(2):
                        to = pl.multiple_of(((store ^ (4 * d + 2 * h)) + o) * sub, sub)
                        at = (2 * h + o) * sub
                        a_ref[pl.ds(to, sub), :] = items[d][at : at + sub, :]
            for e in range(4):
                for d in range(4):
                    to = pl.multiple_of((item ^ (4 * e + d)) * share, share)
                    at = (2 * d + which) * share
                    b_ref[pl.ds(to, share), :] = stores[e][at : at + share, :]
            for h in range(2):
                at = (2 * h + which) * sub
                near_a[h * sub : (h + 1) * sub, :] = items[0][at : at + sub, :]
            for d in range(4):
                at = (2 * d + which) * share
                near_b[d * share : (d + 1) * share, :] = stores[0][at : at + share, :]
            for ref in weeks_ref:
                ref[...] = tree([item[rows:, :] for item in items])


def far_gather(sub, share, value, weeks):
    rank = value.shape[1]
    rows = [value] + [chip_swap(value, d, d) for d in OUTER]
    outs = [(16 * sub, rank), (16 * share, rank), (2 * sub, rank), (4 * share, rank)]
    outs = outs + ([(weeks, rank)] if weeks else [])
    others = [swap(row, "store", CORE) for row in rows]
    return small_call(functools.partial(unstack_kernel, sub, share), outs, *rows[::-1], *others[::-1])


def pack_kernel(used, gbt_ref, mine_ref, core_ref, *refs):
    outs, gb = refs[:4], refs[4]
    gb[...] = gbt_ref[...].T
    share = gb.shape[0] // 16
    more = used - 4 * share
    for e, out in enumerate(outs):
        for d in range(4):
            out[d * share : (d + 1) * share, :] = gb[pl.ds(row_of("item", share, 4 * e + d), share), :]
        out[4 * share : used, :] = mine_ref[:more, :] + core_ref[:more, :]
        if out.shape[0] > used:
            out[used:, :] = jnp.zeros((out.shape[0] - used, out.shape[1]), F32)


def pack_call(gbt, mine, core, used, rows):
    rank, n_stores = gbt.shape
    return pl.pallas_call(
        functools.partial(pack_kernel, used),
        out_shape=[jax.ShapeDtypeStruct((rows, rank), F32)] * 4,
        in_specs=[VM] * 3,
        out_specs=[VM] * 4,
        scratch_shapes=[pltpu.VMEM((n_stores, rank), F32)],
        compiler_params=pltpu.CompilerParams(vmem_limit_bytes=8 * MIB),
        cost_estimate=pl.CostEstimate(flops=LONG, bytes_accessed=0, transcendentals=0),
    )(gbt, mine, core)


def core_sum_kernel(own_ref, got_ref, *outs):
    rows = outs[0].shape[0]
    for k, out in enumerate(outs):
        part = slice(k * rows, (k + 1) * rows)
        out[...] = own_ref[part, :] + got_ref[part, :]


def sum_after_kernel(*refs):
    refs[-1][...] = tree([ref[...] for ref in refs[:-2]])


def sum_kernel(*refs):
    rows = refs[-1].shape[0]
    refs[-1][...] = tree([ref[:rows, :] for ref in refs[:-1]])


def mid_kernel(rate_a, rate_b, share, x0, z3, z2, z1, oldb_ref, mine, got, olda_ref, out_ref):
    terms = (x0, z1, z2, z3)
    n = mine.shape[0]
    half = n // 2
    first = n + x0.shape[0] - 4 * share
    for k in range(4):
        total = tree([t[(k ^ d) * share : ((k ^ d) + 1) * share, :] for d, t in enumerate(terms)])
        part = slice(k * share, (k + 1) * share)
        out_ref[first + k * share : first + (k + 1) * share, :] = oldb_ref[part, :] - rate_b * total
    out_ref[:half, :] = olda_ref[:half, :] - rate_a * (mine[:half, :] + got[half:, :])
    out_ref[half:n, :] = olda_ref[half:, :] - rate_a * (mine[half:, :] + got[:half, :])
    out_ref[n:first, :] = tree([t[4 * share :, :] for t in terms])


def deal_kernel(share, q0, r1, r2, r3, *outs):
    for d, out in enumerate(outs):
        part = slice(d * share, (d + 1) * share)
        out[:share, :] = (q0[part, :] + r1[part, :]) + (r2[part, :] + r3[part, :])
        out[share:, :] = (q0[4 * share :, :] + r1[4 * share :, :]) + (r2[4 * share :, :] + r3[4 * share :, :])


def halves_kernel(t0, u1, u2, u3, after_ref, keep_ref, send_ref):
    half = keep_ref.shape[0]
    grad = (t0[...] + u1[...]) + (u2[...] + u3[...])
    keep_ref[...] = grad[:half, :]
    send_ref[...] = grad[half:, :]


def last_kernel(d0, z1, z2, z3, grad_ref, weeks_ref):
    share = grad_ref.shape[0]
    total = (d0[...] + z1[...]) + (z2[...] + z3[...])
    grad_ref[...] = total[:share, :]
    weeks_ref[...] = total[share:, :]


def end_kernel(rate_a, rate_b, rate_c, count, *refs):
    keep, got, old_ref, e0, e3, e2, e1, c_ref, gradb_ref, b_ref, newa_ref, newb_ref, newc_ref, loss_ref = refs
    newb_ref[...] = b_ref[: newb_ref.shape[0], :] - rate_b * gradb_ref[...]
    newa_ref[...] = old_ref[: keep.shape[0], :] - rate_a * (keep[...] + got[...])
    total = (e0[...] + e1[...]) + (e2[...] + e3[...])
    weeks = c_ref.shape[0]
    newc_ref[...] = c_ref[...] - rate_c * total[:weeks, :]
    for k in range(2):
        loss_ref[k] = jnp.sum(total[weeks + k : weeks + k + 1, :]) / count


def body(sales, launch_week, open_week, item_factors, store_factors, week_factors):
    weeks, n_items, n_stores = sales.shape
    total_items = n_items * lax.axis_size("item")
    total_stores = n_stores * lax.axis_size("store")
    count = total_items * total_stores * weeks
    rate_a = 40.0 / (total_stores * weeks)
    rate_b = 40.0 / (total_items * weeks)
    rate_c = 40.0 / (total_items * total_stores)
    sub, rank = item_factors.shape
    share = store_factors.shape[0]
    pair, quarter = (2 * sub, rank), (4 * share, rank)

    def over(values, axis, partners):
        return [swap(v, axis, d) for v, d in zip(values, partners)]

    other_a = swap(item_factors, "store", CORE)
    other_b = swap(store_factors, "store", CORE)
    own, own_b, late = pl.pallas_call(
        prepare_kernel,
        out_shape=[
            jax.ShapeDtypeStruct((sub, rank), F32),
            jax.ShapeDtypeStruct((share, rank), F32),
            jax.ShapeDtypeStruct((n_items, n_stores), jnp.int32),
        ],
        in_specs=[pl.BlockSpec(memory_space=pltpu.HBM)] * 4,
        out_specs=[VM] * 3,
        scratch_shapes=[
            pltpu.VMEM((n_items // rank, rank), jnp.int32),
            pltpu.VMEM((1, n_stores), jnp.int32),
            pltpu.SemaphoreType.DMA((4,)),
        ],
        compiler_params=pltpu.CompilerParams(vmem_limit_bytes=8 * MIB),
    )(*[
        pltpu.with_memory_space_constraint(x, pltpu.HBM)
        for x in (item_factors, store_factors, launch_week.reshape(-1, rank), open_week.reshape(1, -1))
    ])
    z1, z2 = small_call(near_kernel, [pair, (2 * share, rank)], own, other_a, own_b, other_b)
    near = [chip_swap(z1, ZHI, 1), chip_swap(z2, 0, 2), chip_swap(z2, 0, 3)]
    (value,) = small_call(join_kernel, [(4 * sub, rank)], z1, z2, *near[::-1], flops=LONG)
    block_a, block_b, mine_a, mine_b = far_gather(sub, share, value, 0)
    old = jnp.zeros((weeks + 8, rank), F32)
    errors, gbt, old, factor_c = step_call(rate_c, False, sales, late, block_a, block_b, week_factors, old)

    got_c = swap(old, "store", ZHI)
    send, own = items_grad_call(errors, block_b, factor_c, old)
    parts = small_call(core_sum_kernel, [pair] * 4, own, swap(send, "store", CORE))
    parts = [parts[0]] + over(parts[1:], "store", OUTER)
    dealt = pack_call(gbt, old, got_c, 4 * share + weeks, 2 * sub + weeks)
    dealt = [dealt[0]] + over(dealt[1:], "item", OUTER)
    (part_a,) = small_call(sum_after_kernel, [pair], *parts, dealt[0])
    got_a = swap(part_a, "store", ZHI)
    (part_b,) = small_call(sum_kernel, [(4 * share + weeks, rank)], *dealt)
    near = over([part_b] * 3, "item", ZLOS)
    (new,) = small_call(
        functools.partial(mid_kernel, rate_a, rate_b, share),
        [(2 * sub + weeks + 4 * share, rank)],
        part_b, *near[::-1], mine_b, part_a, got_a, mine_a,
    )
    (value,) = small_call(
        functools.partial(merge_kernel, sub, share), [(4 * sub + weeks, rank)], new, swap(new, "store", CORE)
    )
    block_a, block_b, mine_a, mine_b, grad_c = far_gather(sub, share, value, weeks)
    errors, gbt, old, factor_c = step_call(rate_c, True, sales, late, block_a, block_b, factor_c, old, grad_c)

    (part_c,) = small_call(sum_kernel, [(weeks + 8, rank)], old, swap(old, "store", CORE))
    got_c = swap(part_c, "store", ZHI)
    send, own = items_grad_call(errors, block_b, factor_c, part_c)
    parts = small_call(core_sum_kernel, [pair] * 4, own, swap(send, "store", CORE))
    parts = [parts[0]] + over(parts[1:], "store", OUTER)
    dealt = pack_call(gbt, part_c, got_c, 4 * share + weeks + 8, 4 * share + weeks + 8)
    dealt = [dealt[0]] + over(dealt[1:], "item", OUTER)
    keep, send = small_call(halves_kernel, [(sub, rank)] * 2, *parts, dealt[0])
    got_a = swap(send, "store", ZHI)
    near = small_call(functools.partial(deal_kernel, share), [(share + weeks + 8, rank)] * 4, *dealt)
    near = [near[0]] + over(near[1:], "item", ZLOS)
    grad_b, part_c = small_call(last_kernel, [(share, rank), (weeks + 8, rank)], *near)
    shard_a, shard_b, factor_c, losses = pl.pallas_call(
        functools.partial(end_kernel, rate_a, rate_b, rate_c, 2.0 * count),
        out_shape=[jax.ShapeDtypeStruct(s, F32) for s in ((sub, rank), (share, rank), (weeks, rank), (2,))],
        in_specs=[VM] * 10,
        out_specs=[VM, VM, VM, pl.BlockSpec(memory_space=pltpu.SMEM)],
        compiler_params=pltpu.CompilerParams(vmem_limit_bytes=8 * MIB),
        cost_estimate=pl.CostEstimate(flops=0, bytes_accessed=0, transcendentals=0),
    )(keep, got_a, mine_a, part_c, *over([part_c] * 3, "store", OUTER)[::-1], factor_c, grad_b, mine_b)
    return shard_a, shard_b, factor_c, losses


def solution(mesh):
    in_specs = (
        P(None, "item", "store"),
        P("item"),
        P("store"),
        P(("item", "store"), None),
        P(("store", "item"), None),
        P(),
    )
    out_specs = (P(("item", "store"), None), P(("store", "item"), None), P(), P())
    return jax.shard_map(body, mesh=mesh, in_specs=in_specs, out_specs=out_specs, check_vma=False)
```
